32 devices in a mesh: groups: 2 (over x), dp: 16 (over z, y, core).
Axes of the slice: x: 2, y: 2, z: 4, core: 2. Of those that a mesh axis runs over, the one named last changes fastest.
Arguments:
- embeddings: bfloat16 [4096, 1024], P(('groups', 'dp')), parts along dimension 0
- cluster_ids: int32 [4096], P(('groups', 'dp')), parts along dimension 0, may hold values from 0 to 511, as said below
- owner: int32 [1024], P('groups'), parts along dimension 0, may hold values from 0 to 15, as said below
Outputs:
- smoothed: bfloat16 [4096, 1024], P(('groups', 'dp')), parts along dimension 0
The draws below stay inside these ranges and needn't reach their ends.
There are 2 independent parts, one for each index of `groups`. The reference program is written for one: setup_inputs(seed, part) draws one part's arguments, and reference() takes and returns one part's arrays. A program takes and returns all parts, laid end to end along the dimension named above; each array names one. Nothing has to cross between parts.
Inputs may be any that keep to these rules, and one draw needn't show every extreme that they name: `owner`: every device number owns exactly 32 clusters. `cluster_ids`: among the rows of one device, at most 16 belong to clusters of one owner, and on every device some owner gets exactly 16 of them.
All inputs are finite; a program needn't handle non-finite values.
Results may differ from the reference program's by a relative error of at most 0.0041.
Values may be sent and summed in bfloat16 or wider, within the bound.
A program may use at most 64 MiB of HBM per device.

```python
import jax
import jax.numpy as jnp
from jax import lax

D = 1024
ROW_DEV = 128
CLU_DEV = 32
CLUSTERS = 512
ROWS = 2048
SLOT = 16
N_DP = 16


def owner_perm(key):
    return jax.random.permutation(jax.random.fold_in(key, 11), CLUSTERS)


def row_clusters(key):
    perm = owner_perm(key)
    total = N_DP * SLOT
    boost = jax.random.randint(jax.random.fold_in(key, 12), (N_DP,), 0, 4) * (1 << 17)
    slot_owner = jnp.arange(total, dtype=jnp.int32) // SLOT

    def one_source(source_index):
        split_key = jax.random.fold_in(jax.random.fold_in(key, 13), source_index)
        first_block, latter_tile, third_block, fourth_block = jax.random.split(split_key, 4)
        score = jax.random.randint(first_block, (total,), 0, 1 << 18) + boost[slot_owner]
        selected_holder = jax.random.randint(latter_tile, (), 0, N_DP)
        score = jnp.where(slot_owner == selected_holder, -1, score)
        chosen = jnp.argsort(score, stable=True)[:ROW_DEV]
        target = jax.random.permutation(third_block, chosen // SLOT)
        local = jax.random.randint(fourth_block, (ROW_DEV,), 0, CLU_DEV)
        return perm[target * CLU_DEV + local]
    return jax.vmap(one_source)(jnp.arange(N_DP, dtype=jnp.int32)).reshape(ROWS).astype(jnp.int32)


def draw_owner(key, part):
    return (jnp.argsort(owner_perm(key)) // CLU_DEV).astype(jnp.int32)


def draw_cluster_ids(key, part):
    return row_clusters(key)


def draw_embeddings(key, part):
    labels = row_clusters(key)
    ckey = jax.random.fold_in(key, 14)
    centers = jax.vmap(lambda label: jax.random.normal(jax.random.fold_in(ckey, label), (D,), jnp.float32))(labels)
    mkey, nkey = jax.random.split(jax.random.fold_in(key, 15), 2)
    mixing = jax.random.uniform(mkey, (ROWS, 1), jnp.float32, 0.35, 1.0)
    noise = jax.random.normal(nkey, (ROWS, D), jnp.float32)
    values = mixing * centers + jnp.sqrt(1.0 - mixing * mixing) * noise
    return values.astype(jnp.bfloat16)


def setup_inputs(seed: int = 0, part: int = 0) -> dict:
    splits = jax.random.split(jax.random.key(seed), 4)
    own_keys = jax.random.split(jax.random.fold_in(splits[3], part), 4)
    embeddings = draw_embeddings(jax.random.fold_in(jax.random.fold_in(splits[3], part), 71), part)
    cluster_ids = draw_cluster_ids(jax.random.fold_in(jax.random.fold_in(splits[3], part), 71), part)
    owner = draw_owner(jax.random.fold_in(jax.random.fold_in(splits[3], part), 71), part)
    return {"embeddings": embeddings, "cluster_ids": cluster_ids, "owner": owner}


epsilon = 1e-06
sharpness_scale = 0.25

def smooth_rows(rows, labels):
    values = rows.astype(jnp.float32)
    unit = (values * lax.rsqrt(lax.optimization_barrier(jnp.sum(values * values, axis=1, keepdims=True)) + epsilon)).astype(jnp.bfloat16)
    pairwise_similarity = jnp.dot(unit, unit.T, preferred_element_type=jnp.float32)
    shared_group_filter = (labels[:, None] == labels[None, :]) & (labels[:, None] >= 0)
    affinity_factor = jnp.where(shared_group_filter, jnp.exp((pairwise_similarity - 1.0) / sharpness_scale), jnp.float32(0.0))
    total = lax.optimization_barrier(jnp.sum(affinity_factor, axis=1))
    numer = jnp.dot(affinity_factor.astype(jnp.bfloat16), rows, preferred_element_type=jnp.float32)
    total = jnp.where(labels >= 0, total, jnp.float32(1.0))
    return (numer / total[:, None]).astype(jnp.bfloat16)

def reference(embeddings, cluster_ids, owner):
    dest = jnp.take(owner, cluster_ids).astype(jnp.int32)
    by_source = dest.reshape(N_DP, ROW_DEV)
    onehot = (by_source[:, :, None] == jnp.arange(N_DP, dtype=jnp.int32)[None, None, :]).astype(jnp.int32)
    rank = lax.optimization_barrier(jnp.sum(onehot * (jnp.cumsum(onehot, axis=1) - 1), axis=2)).astype(jnp.int32)
    source_index = jnp.arange(N_DP, dtype=jnp.int32)[:, None] * SLOT + rank
    table = jnp.full((N_DP, N_DP * SLOT), ROWS, jnp.int32)
    table = table.at[by_source.reshape(-1), source_index.reshape(-1)].set(jnp.arange(ROWS, dtype=jnp.int32))

    def per_owner(indices):
        valid = indices < ROWS
        safe = jnp.minimum(indices, ROWS - 1)
        rows = jnp.where(valid[:, None], embeddings[safe], jnp.zeros((), jnp.bfloat16))
        labels = jnp.where(valid, cluster_ids[safe], -1).astype(jnp.int32)
        return smooth_rows(rows, labels)
    results = lax.map(per_owner, table)
    output = jnp.zeros((ROWS, D), jnp.bfloat16)
    return output.at[table.reshape(-1)].set(results.reshape(-1, D), mode='drop')
```

```python
import functools

import jax
import jax.numpy as jnp
from jax import lax
from jax.experimental import pallas as pl
from jax.experimental.pallas import tpu as pltpu
from jax.sharding import PartitionSpec as P

epsilon = 1e-06
sharpness_scale = 0.25
ROW_TILE = 16


def normalize(rows):
    values = rows.astype(jnp.float32)
    return (values * lax.rsqrt(jnp.sum(values * values, axis=1, keepdims=True) + epsilon)).astype(
        jnp.bfloat16
    )


def kernel_terms(query_unit, query_labels, key_unit, compared_group_ids, key_rows):
    pairwise_similarity = jnp.dot(query_unit, key_unit.T, preferred_element_type=jnp.float32)
    shared_group_filter = (query_labels[:, None] == compared_group_ids[None, :]) & (
        query_labels[:, None] >= 0
    )
    affinity_factor = jnp.where(
        shared_group_filter,
        jnp.exp((pairwise_similarity - 1.0) / sharpness_scale),
        jnp.float32(0.0),
    )
    total = jnp.sum(affinity_factor, axis=1)
    numer = jnp.dot(
        affinity_factor.astype(jnp.bfloat16), key_rows, preferred_element_type=jnp.float32
    )
    return (numer, total)


def finish(numer, total, labels):
    total = jnp.where(labels >= 0, total, jnp.float32(1.0))
    return (numer / total[:, None]).astype(jnp.bfloat16)


def by_collectives(embeddings, cluster_ids, owner):
    peers = lax.axis_size("dp")
    rows_dev, width = embeddings.shape
    slot = 2 * rows_dev // peers
    dest = jnp.take(owner, cluster_ids)
    onehot = (dest[:, None] == jnp.arange(peers, dtype=jnp.int32)[None, :]).astype(jnp.int32)
    rank = jnp.sum(onehot * (jnp.cumsum(onehot, axis=0) - 1), axis=1)
    target = dest * slot + rank
    outgoing = (
        jnp.zeros((peers * slot, width), jnp.bfloat16)
        .at[target]
        .set(embeddings)
        .reshape(peers, slot, width)
    )
    labels = (
        jnp.full((peers * slot,), -1, jnp.int32).at[target].set(cluster_ids).reshape(peers, slot)
    )
    received, got_labels = (
        lax.all_to_all(outgoing, "dp", split_axis=0, concat_axis=0, tiled=True),
        lax.all_to_all(labels, "dp", split_axis=0, concat_axis=0, tiled=True),
    )
    flat_rows = received.reshape(-1, width)
    flat_labels = got_labels.reshape(-1)
    unit = normalize(flat_rows)
    numer, total = kernel_terms(unit, flat_labels, unit, flat_labels, flat_rows)
    result = finish(numer, total, flat_labels).reshape(peers, slot, width)
    back = lax.all_to_all(result, "dp", split_axis=0, concat_axis=0, tiled=True)
    return back.reshape(-1, width)[target]


def iota(shape, axis):
    return lax.broadcasted_iota(jnp.int32, shape, axis)


def smooth_kernel(
    peers, slot, emb_hbm, ids_ref, owner_ref, out_ref,
    emb, sent, got, unit, made, back, place, lab_out, lab_in,
    emb_sem, lab_send, lab_recv, row_send, row_recv, back_send, back_recv,
):
    rows_dev, width = emb.shape
    clusters = owner_ref.shape[1]
    slots = peers * slot
    me = lax.axis_index("dp")
    load = pltpu.make_async_copy(emb_hbm, emb, emb_sem)
    load.start()

    barrier = pltpu.get_barrier_semaphore()
    for k in range(1, peers):
        pl.semaphore_signal(
            barrier, inc=1, device_id={"dp": lax.rem(me + k, peers)},
            device_id_type=pl.DeviceIdType.MESH,
        )

    order = sorted(range(1, peers), key=lambda k: abs(k - peers // 2))

    def remote(src, dst, send, recv, k, forward):
        peer = lax.rem(me + (k if forward else peers - k), peers)
        return pltpu.make_async_remote_copy(
            src_ref=src, dst_ref=dst, send_sem=send.at[k], recv_sem=recv.at[k],
            device_id={"dp": peer}, device_id_type=pl.DeviceIdType.MESH,
        )

    def block(ref, k):
        return ref.at[pl.ds(k * slot, slot)]

    lab_copy = {
        k: remote(lab_out, lab_in.at[k], lab_send, lab_recv, k, True) for k in order
    }
    row_copy = {
        k: remote(block(sent, k), block(got, k), row_send, row_recv, k, True) for k in order
    }
    back_copy = {
        k: remote(block(made, k), block(back, k), back_send, back_recv, k, False) for k in order
    }

    ids = ids_ref[...]
    which = (iota((clusters, rows_dev), 0) == ids).astype(jnp.bfloat16)
    owners = jnp.broadcast_to(owner_ref[...].astype(jnp.bfloat16), (8, clusters))
    dest = jnp.dot(owners, which, preferred_element_type=jnp.float32)[:1].astype(jnp.int32)
    ahead = dest - me
    ahead = jnp.where(ahead < 0, ahead + peers, ahead)
    hit = iota((peers, rows_dev), 0) == ahead
    earlier = (iota((rows_dev, rows_dev), 0) < iota((rows_dev, rows_dev), 1)).astype(jnp.bfloat16)
    count = jnp.dot(hit.astype(jnp.bfloat16), earlier, preferred_element_type=jnp.float32)
    rank = jnp.sum(jnp.where(hit, count, 0.0), axis=0, keepdims=True).astype(jnp.int32)
    target = ahead * slot + rank
    put = (iota((slots, rows_dev), 0) == target).astype(jnp.bfloat16)
    place[...] = put

    row8 = iota((8, rows_dev), 0)
    high = ids // 64
    parts = jnp.where(row8 == 0, high, jnp.where(row8 == 1, ids - 64 * high, 1))
    spread = lax.dot_general(
        parts.astype(jnp.bfloat16), put, (((1,), (1,)), ((), ())),
        preferred_element_type=jnp.float32,
    )
    labels = (64.0 * spread[0:1] + spread[1:2] + (spread[2:3] - 1.0)).astype(jnp.int32)
    lab_out[...] = labels
    lab_in[0] = labels

    far = slice(slots // 4, 3 * slots // 4)
    groups = [far, slice(0, slots // 4), slice(3 * slots // 4, slots)]

    def inside(part):
        return [k for k in order if part.start <= k * slot < part.stop]

    load.wait()
    pl.semaphore_wait(barrier, peers - 1)
    for k in order:
        lab_copy[k].start()
    for part in groups:
        sent[part, :] = jnp.dot(
            place[part, :], emb[...], preferred_element_type=jnp.float32
        ).astype(jnp.bfloat16)
        for k in inside(part):
            row_copy[k].start()
    got[:slot, :] = sent[:slot, :]
    unit[:slot, :] = normalize(got[:slot, :])

    for k in order:
        lab_copy[k].wait_recv()
    lane = iota((1, slots), 1)
    label_row = lab_in[0]
    for k in range(1, peers):
        label_row = jnp.where(lane >= k * slot, lab_in[k], label_row)
    square = iota((slots, slots), 0) == iota((slots, slots), 1)
    label_col = jnp.sum(jnp.where(square, label_row, 0), axis=1, keepdims=True)
    same = label_col == label_row

    for k in reversed(order):
        row_copy[k].wait_recv()
        here = slice(k * slot, (k + 1) * slot)
        unit[here, :] = normalize(got[here, :])

    gram = lax.dot_general(
        unit[...], unit[...], (((1,), (1,)), ((), ())), preferred_element_type=jnp.float32
    )
    weight = jnp.where(same, jnp.exp((gram - 1.0) / sharpness_scale), 0.0)
    total = jnp.sum(weight, axis=1, keepdims=True)
    weight_b = weight.astype(jnp.bfloat16)
    for part in groups:
        numer = jnp.dot(weight_b[part], got[...], preferred_element_type=jnp.float32)
        made[part, :] = (numer / total[part]).astype(jnp.bfloat16)
        for k in inside(part):
            back_copy[k].start()
    back[:slot, :] = made[:slot, :]

    for k in reversed(order):
        back_copy[k].wait_recv()
    out_ref[...] = lax.dot_general(
        place[...], back[...], (((0,), (0,)), ((), ())), preferred_element_type=jnp.float32
    ).astype(out_ref.dtype)
    for k in order:
        lab_copy[k].wait_send()
        row_copy[k].wait_send()
        back_copy[k].wait_send()


def by_kernel(embeddings, cluster_ids, owner):
    peers = lax.axis_size("dp")
    rows_dev, width = embeddings.shape
    slot = 2 * rows_dev // peers
    slots = peers * slot
    sems = pltpu.SemaphoreType.DMA((peers,))
    vmem = pl.BlockSpec(memory_space=pltpu.VMEM)
    return pl.pallas_call(
        functools.partial(smooth_kernel, peers, slot),
        out_shape=jax.ShapeDtypeStruct((rows_dev, width), jnp.bfloat16),
        in_specs=[pl.BlockSpec(memory_space=pl.ANY), vmem, vmem],
        out_specs=vmem,
        scratch_shapes=[
            pltpu.VMEM((rows_dev, width), jnp.bfloat16),
            pltpu.VMEM((slots, width), jnp.bfloat16),
            pltpu.VMEM((slots, width), jnp.bfloat16),
            pltpu.VMEM((slots, width), jnp.bfloat16),
            pltpu.VMEM((slots, width), jnp.bfloat16),
            pltpu.VMEM((slots, width), jnp.bfloat16),
            pltpu.VMEM((slots, rows_dev), jnp.bfloat16),
            pltpu.VMEM((1, slots), jnp.int32),
            pltpu.VMEM((peers, 1, slots), jnp.int32),
            pltpu.SemaphoreType.DMA,
            sems, sems, sems, sems, sems, sems,
        ],
        compiler_params=pltpu.CompilerParams(
            collective_id=0, has_side_effects=True, vmem_limit_bytes=32 * 1024 * 1024
        ),
    )(embeddings, cluster_ids.reshape(1, rows_dev), owner.reshape(1, -1))


def shards(embeddings, cluster_ids, owner):
    slot = 2 * embeddings.shape[0] // lax.axis_size("dp")
    if slot % ROW_TILE == 0:
        return by_kernel(embeddings, cluster_ids, owner)
    return by_collectives(embeddings, cluster_ids, owner)


def solution(mesh):
    placed = (P(("groups", "dp"), None), P(("groups", "dp")), P("groups"))
    return jax.shard_map(
        shards, mesh=mesh, in_specs=placed, out_specs=P(("groups", "dp"), None), check_vma=False
    )
```

```python
import functools

import jax
import jax.numpy as jnp
from jax import lax
from jax.experimental import pallas as pl
from jax.experimental.pallas import tpu as pltpu
from jax.sharding import PartitionSpec as P

epsilon = 1e-06
sharpness_scale = 0.25
ROW_TILE = 16


def normalize(rows):
    values = rows.astype(jnp.float32)
    return (values * lax.rsqrt(jnp.sum(values * values, axis=1, keepdims=True) + epsilon)).astype(
        jnp.bfloat16
    )


def kernel_terms(query_unit, query_labels, key_unit, compared_group_ids, key_rows):
    pairwise_similarity = jnp.dot(query_unit, key_unit.T, preferred_element_type=jnp.float32)
    shared_group_filter = (query_labels[:, None] == compared_group_ids[None, :]) & (
        query_labels[:, None] >= 0
    )
    affinity_factor = jnp.where(
        shared_group_filter,
        jnp.exp((pairwise_similarity - 1.0) / sharpness_scale),
        jnp.float32(0.0),
    )
    total = jnp.sum(affinity_factor, axis=1)
    numer = jnp.dot(
        affinity_factor.astype(jnp.bfloat16), key_rows, preferred_element_type=jnp.float32
    )
    return (numer, total)


def finish(numer, total, labels):
    total = jnp.where(labels >= 0, total, jnp.float32(1.0))
    return (numer / total[:, None]).astype(jnp.bfloat16)


def by_collectives(embeddings, cluster_ids, owner):
    peers = lax.axis_size("dp")
    rows_dev, width = embeddings.shape
    slot = 2 * rows_dev // peers
    dest = jnp.take(owner, cluster_ids)
    onehot = (dest[:, None] == jnp.arange(peers, dtype=jnp.int32)[None, :]).astype(jnp.int32)
    rank = jnp.sum(onehot * (jnp.cumsum(onehot, axis=0) - 1), axis=1)
    target = dest * slot + rank
    outgoing = (
        jnp.zeros((peers * slot, width), jnp.bfloat16)
        .at[target]
        .set(embeddings)
        .reshape(peers, slot, width)
    )
    labels = (
        jnp.full((peers * slot,), -1, jnp.int32).at[target].set(cluster_ids).reshape(peers, slot)
    )
    received, got_labels = (
        lax.all_to_all(outgoing, "dp", split_axis=0, concat_axis=0, tiled=True),
        lax.all_to_all(labels, "dp", split_axis=0, concat_axis=0, tiled=True),
    )
    flat_rows = received.reshape(-1, width)
    flat_labels = got_labels.reshape(-1)
    unit = normalize(flat_rows)
    numer, total = kernel_terms(unit, flat_labels, unit, flat_labels, flat_rows)
    result = finish(numer, total, flat_labels).reshape(peers, slot, width)
    back = lax.all_to_all(result, "dp", split_axis=0, concat_axis=0, tiled=True)
    return back.reshape(-1, width)[target]


def iota(shape, axis):
    return lax.broadcasted_iota(jnp.int32, shape, axis)


def smooth_kernel(
    peers, slot, emb_hbm, ids_ref, owner_ref, out_ref,
    emb, sent, got, unit, made, back, place, lab_out, lab_in,
    emb_sem, lab_send, lab_recv, row_send, row_recv, back_send, back_recv,
):
    rows_dev, width = emb.shape
    clusters = owner_ref.shape[1]
    slots = peers * slot
    me = lax.axis_index("dp")
    load = pltpu.make_async_copy(emb_hbm, emb, emb_sem)
    load.start()

    barrier = pltpu.get_barrier_semaphore()
    for k in range(1, peers):
        pl.semaphore_signal(
            barrier, inc=1, device_id={"dp": lax.rem(me + k, peers)},
            device_id_type=pl.DeviceIdType.MESH,
        )

    order = sorted(range(1, peers), key=lambda k: -abs(k - peers // 2))

    def remote(src, dst, send, recv, k, forward):
        peer = lax.rem(me + (k if forward else peers - k), peers)
        return pltpu.make_async_remote_copy(
            src_ref=src, dst_ref=dst, send_sem=send.at[k], recv_sem=recv.at[k],
            device_id={"dp": peer}, device_id_type=pl.DeviceIdType.MESH,
        )

    def block(ref, k):
        return ref.at[pl.ds(k * slot, slot)]

    lab_copy = {
        k: remote(lab_out, lab_in.at[k], lab_send, lab_recv, k, True) for k in order
    }
    row_copy = {
        k: remote(block(sent, k), block(got, k), row_send, row_recv, k, True) for k in order
    }
    back_copy = {
        k: remote(block(made, k), block(back, k), back_send, back_recv, k, False) for k in order
    }

    ids = ids_ref[...]
    which = (iota((clusters, rows_dev), 0) == ids).astype(jnp.bfloat16)
    owners = jnp.broadcast_to(owner_ref[...].astype(jnp.bfloat16), (8, clusters))
    dest = jnp.dot(owners, which, preferred_element_type=jnp.float32)[:1].astype(jnp.int32)
    ahead = dest - me
    ahead = jnp.where(ahead < 0, ahead + peers, ahead)
    hit = iota((peers, rows_dev), 0) == ahead
    earlier = (iota((rows_dev, rows_dev), 0) < iota((rows_dev, rows_dev), 1)).astype(jnp.bfloat16)
    count = jnp.dot(hit.astype(jnp.bfloat16), earlier, preferred_element_type=jnp.float32)
    rank = jnp.sum(jnp.where(hit, count, 0.0), axis=0, keepdims=True).astype(jnp.int32)
    target = ahead * slot + rank
    put = (iota((slots, rows_dev), 0) == target).astype(jnp.bfloat16)
    place[...] = put

    row8 = iota((8, rows_dev), 0)
    high = ids // 64
    parts = jnp.where(row8 == 0, high, jnp.where(row8 == 1, ids - 64 * high, 1))
    spread = lax.dot_general(
        parts.astype(jnp.bfloat16), put, (((1,), (1,)), ((), ())),
        preferred_element_type=jnp.float32,
    )
    labels = (64.0 * spread[0:1] + spread[1:2] + (spread[2:3] - 1.0)).astype(jnp.int32)
    lab_out[...] = labels
    lab_in[0] = labels

    far = slice(slots // 4, 3 * slots // 4)
    groups = [slice(0, slots // 4), slice(3 * slots // 4, slots), far]

    def inside(part):
        return [k for k in order if part.start <= k * slot < part.stop]

    load.wait()
    pl.semaphore_wait(barrier, peers - 1)
    for k in order:
        lab_copy[k].start()
    for part in groups:
        sent[part, :] = jnp.dot(
            place[part, :], emb[...], preferred_element_type=jnp.float32
        ).astype(jnp.bfloat16)
        for k in inside(part):
            row_copy[k].start()
    got[:slot, :] = sent[:slot, :]
    unit[:slot, :] = normalize(got[:slot, :])

    for k in order:
        lab_copy[k].wait_recv()
    lane = iota((1, slots), 1)
    label_row = lab_in[0]
    for k in range(1, peers):
        label_row = jnp.where(lane >= k * slot, lab_in[k], label_row)
    square = iota((slots, slots), 0) == iota((slots, slots), 1)
    label_col = jnp.sum(jnp.where(square, label_row, 0), axis=1, keepdims=True)
    same = label_col == label_row

    for k in order:
        row_copy[k].wait_recv()
        here = slice(k * slot, (k + 1) * slot)
        unit[here, :] = normalize(got[here, :])

    gram = lax.dot_general(
        unit[...], unit[...], (((1,), (1,)), ((), ())), preferred_element_type=jnp.float32
    )
    weight = jnp.where(same, jnp.exp((gram - 1.0) / sharpness_scale), 0.0)
    inverse = 1.0 / jnp.sum(weight, axis=1, keepdims=True)
    weight_b = weight.astype(jnp.bfloat16)
    for part in groups:
        numer = jnp.dot(weight_b[part], got[...], preferred_element_type=jnp.float32)
        made[part, :] = (numer * inverse[part]).astype(jnp.bfloat16)
        for k in inside(part):
            back_copy[k].start()
    back[:slot, :] = made[:slot, :]

    for k in order:
        lab_copy[k].wait_send()
        row_copy[k].wait_send()
    rows = jnp.zeros((rows_dev, width), jnp.float32)
    for part in groups:
        for k in inside(part):
            back_copy[k].wait_send()
            back_copy[k].wait_recv()
        rows += lax.dot_general(
            place[part, :], back[part, :], (((0,), (0,)), ((), ())),
            preferred_element_type=jnp.float32,
        )
    out_ref[...] = rows.astype(out_ref.dtype)


def by_kernel(embeddings, cluster_ids, owner):
    peers = lax.axis_size("dp")
    rows_dev, width = embeddings.shape
    slot = 2 * rows_dev // peers
    slots = peers * slot
    sems = pltpu.SemaphoreType.DMA((peers,))
    vmem = pl.BlockSpec(memory_space=pltpu.VMEM)
    return pl.pallas_call(
        functools.partial(smooth_kernel, peers, slot),
        out_shape=jax.ShapeDtypeStruct((rows_dev, width), jnp.bfloat16),
        in_specs=[pl.BlockSpec(memory_space=pl.ANY), vmem, vmem],
        out_specs=vmem,
        scratch_shapes=[
            pltpu.VMEM((rows_dev, width), jnp.bfloat16),
            pltpu.VMEM((slots, width), jnp.bfloat16),
            pltpu.VMEM((slots, width), jnp.bfloat16),
            pltpu.VMEM((slots, width), jnp.bfloat16),
            pltpu.VMEM((slots, width), jnp.bfloat16),
            pltpu.VMEM((slots, width), jnp.bfloat16),
            pltpu.VMEM((slots, rows_dev), jnp.bfloat16),
            pltpu.VMEM((1, slots), jnp.int32),
            pltpu.VMEM((peers, 1, slots), jnp.int32),
            pltpu.SemaphoreType.DMA,
            sems, sems, sems, sems, sems, sems,
        ],
        compiler_params=pltpu.CompilerParams(
            collective_id=0, has_side_effects=True, vmem_limit_bytes=32 * 1024 * 1024
        ),
    )(embeddings, cluster_ids.reshape(1, rows_dev), owner.reshape(1, -1))


def shards(embeddings, cluster_ids, owner):
    slot = 2 * embeddings.shape[0] // lax.axis_size("dp")
    if slot % ROW_TILE == 0:
        return by_kernel(embeddings, cluster_ids, owner)
    return by_collectives(embeddings, cluster_ids, owner)


def solution(mesh):
    placed = (P(("groups", "dp"), None), P(("groups", "dp")), P("groups"))
    return jax.shard_map(
        shards, mesh=mesh, in_specs=placed, out_specs=P(("groups", "dp"), None), check_vma=False
    )
```

```python
import functools

import jax
import jax.numpy as jnp
from jax import lax
from jax.experimental import pallas as pl
from jax.experimental.pallas import tpu as pltpu
from jax.sharding import PartitionSpec as P

epsilon = 1e-06
sharpness_scale = 0.25
ROW_TILE = 16


def normalize(rows):
    values = rows.astype(jnp.float32)
    return (values * lax.rsqrt(jnp.sum(values * values, axis=1, keepdims=True) + epsilon)).astype(
        jnp.bfloat16
    )


def kernel_terms(query_unit, query_labels, key_unit, compared_group_ids, key_rows):
    pairwise_similarity = jnp.dot(query_unit, key_unit.T, preferred_element_type=jnp.float32)
    shared_group_filter = (query_labels[:, None] == compared_group_ids[None, :]) & (
        query_labels[:, None] >= 0
    )
    affinity_factor = jnp.where(
        shared_group_filter,
        jnp.exp((pairwise_similarity - 1.0) / sharpness_scale),
        jnp.float32(0.0),
    )
    total = jnp.sum(affinity_factor, axis=1)
    numer = jnp.dot(
        affinity_factor.astype(jnp.bfloat16), key_rows, preferred_element_type=jnp.float32
    )
    return (numer, total)


def finish(numer, total, labels):
    total = jnp.where(labels >= 0, total, jnp.float32(1.0))
    return (numer / total[:, None]).astype(jnp.bfloat16)


def by_collectives(embeddings, cluster_ids, owner):
    peers = lax.axis_size("dp")
    rows_dev, width = embeddings.shape
    slot = 2 * rows_dev // peers
    dest = jnp.take(owner, cluster_ids)
    onehot = (dest[:, None] == jnp.arange(peers, dtype=jnp.int32)[None, :]).astype(jnp.int32)
    rank = jnp.sum(onehot * (jnp.cumsum(onehot, axis=0) - 1), axis=1)
    target = dest * slot + rank
    outgoing = (
        jnp.zeros((peers * slot, width), jnp.bfloat16)
        .at[target]
        .set(embeddings)
        .reshape(peers, slot, width)
    )
    labels = (
        jnp.full((peers * slot,), -1, jnp.int32).at[target].set(cluster_ids).reshape(peers, slot)
    )
    received, got_labels = (
        lax.all_to_all(outgoing, "dp", split_axis=0, concat_axis=0, tiled=True),
        lax.all_to_all(labels, "dp", split_axis=0, concat_axis=0, tiled=True),
    )
    flat_rows = received.reshape(-1, width)
    flat_labels = got_labels.reshape(-1)
    unit = normalize(flat_rows)
    numer, total = kernel_terms(unit, flat_labels, unit, flat_labels, flat_rows)
    result = finish(numer, total, flat_labels).reshape(peers, slot, width)
    back = lax.all_to_all(result, "dp", split_axis=0, concat_axis=0, tiled=True)
    return back.reshape(-1, width)[target]


def iota(shape, axis):
    return lax.broadcasted_iota(jnp.int32, shape, axis)


def smooth_kernel(
    peers, slot, emb_hbm, ids_ref, owner_ref, out_ref,
    emb, sent, got, unit, made, back, place, lab_out, lab_in,
    emb_sem, lab_send, lab_recv, row_send, row_recv, back_send, back_recv,
):
    rows_dev, width = emb.shape
    clusters = owner_ref.shape[1]
    slots = peers * slot
    me = lax.axis_index("dp")
    load = pltpu.make_async_copy(emb_hbm, emb, emb_sem)
    load.start()

    barrier = pltpu.get_barrier_semaphore()
    for k in range(1, peers):
        pl.semaphore_signal(
            barrier, inc=1, device_id={"dp": lax.rem(me + k, peers)},
            device_id_type=pl.DeviceIdType.MESH,
        )

    order = sorted(range(1, peers), key=lambda k: -abs(k - peers // 2))

    def remote(src, dst, send, recv, k, forward):
        peer = lax.rem(me + (k if forward else peers - k), peers)
        return pltpu.make_async_remote_copy(
            src_ref=src, dst_ref=dst, send_sem=send.at[k], recv_sem=recv.at[k],
            device_id={"dp": peer}, device_id_type=pl.DeviceIdType.MESH,
        )

    def block(ref, k):
        return ref.at[pl.ds(k * slot, slot)]

    lab_copy = {
        k: remote(lab_out, lab_in.at[k], lab_send, lab_recv, k, True) for k in order
    }
    row_copy = {
        k: remote(block(sent, k), block(got, k), row_send, row_recv, k, True) for k in order
    }
    back_copy = {
        k: remote(block(made, k), block(back, k), back_send, back_recv, k, False) for k in order
    }

    ids = ids_ref[...]
    which = (iota((clusters, rows_dev), 0) == ids).astype(jnp.bfloat16)
    owners = jnp.broadcast_to(owner_ref[...].astype(jnp.bfloat16), (8, clusters))
    dest = jnp.dot(owners, which, preferred_element_type=jnp.float32)[:1].astype(jnp.int32)
    ahead = dest - me
    ahead = jnp.where(ahead < 0, ahead + peers, ahead)
    hit = iota((peers, rows_dev), 0) == ahead
    earlier = (iota((rows_dev, rows_dev), 0) < iota((rows_dev, rows_dev), 1)).astype(jnp.bfloat16)
    count = jnp.dot(hit.astype(jnp.bfloat16), earlier, preferred_element_type=jnp.float32)
    rank = jnp.sum(jnp.where(hit, count, 0.0), axis=0, keepdims=True).astype(jnp.int32)
    target = ahead * slot + rank
    put = (iota((slots, rows_dev), 0) == target).astype(jnp.bfloat16)
    place[...] = put

    row8 = iota((8, rows_dev), 0)
    high = ids // 64
    parts = jnp.where(row8 == 0, high, jnp.where(row8 == 1, ids - 64 * high, 1))
    spread = lax.dot_general(
        parts.astype(jnp.bfloat16), put, (((1,), (1,)), ((), ())),
        preferred_element_type=jnp.float32,
    )
    labels = (64.0 * spread[0:1] + spread[1:2] + (spread[2:3] - 1.0)).astype(jnp.int32)
    lab_out[...] = labels
    lab_in[0] = labels

    quarter = slots // 4
    groups = [slice(i * quarter, (i + 1) * quarter) for i in (0, 3, 1, 2)]

    def inside(part):
        return [k for k in order if part.start <= k * slot < part.stop]

    load.wait()
    pl.semaphore_wait(barrier, peers - 1)
    for k in order:
        lab_copy[k].start()
    for part in groups:
        sent[part, :] = jnp.dot(
            place[part, :], emb[...], preferred_element_type=jnp.float32
        ).astype(jnp.bfloat16)
        for k in inside(part):
            row_copy[k].start()
    got[:slot, :] = sent[:slot, :]
    unit[:slot, :] = normalize(got[:slot, :])

    for k in order:
        lab_copy[k].wait_recv()
    lane = iota((1, slots), 1)
    label_row = lab_in[0]
    for k in range(1, peers):
        label_row = jnp.where(lane >= k * slot, lab_in[k], label_row)
    square = iota((slots, slots), 0) == iota((slots, slots), 1)
    label_col = jnp.sum(jnp.where(square, label_row, 0), axis=1, keepdims=True)
    same = label_col == label_row

    for k in order:
        row_copy[k].wait_recv()
        here = slice(k * slot, (k + 1) * slot)
        unit[here, :] = normalize(got[here, :])

    gram = lax.dot_general(
        unit[...], unit[...], (((1,), (1,)), ((), ())), preferred_element_type=jnp.float32
    )
    weight = jnp.where(same, jnp.exp((gram - 1.0) / sharpness_scale), 0.0)
    inverse = 1.0 / jnp.sum(weight, axis=1, keepdims=True)
    weight_b = weight.astype(jnp.bfloat16)
    for part in groups:
        numer = jnp.dot(weight_b[part], got[...], preferred_element_type=jnp.float32)
        made[part, :] = (numer * inverse[part]).astype(jnp.bfloat16)
        for k in inside(part):
            back_copy[k].start()
    back[:slot, :] = made[:slot, :]

    for k in order:
        lab_copy[k].wait_send()
        row_copy[k].wait_send()
    rows = jnp.zeros((rows_dev, width), jnp.float32)
    for part in groups:
        for k in inside(part):
            back_copy[k].wait_send()
            back_copy[k].wait_recv()
        rows += lax.dot_general(
            place[part, :], back[part, :], (((0,), (0,)), ((), ())),
            preferred_element_type=jnp.float32,
        )
    out_ref[...] = rows.astype(out_ref.dtype)


def by_kernel(embeddings, cluster_ids, owner):
    peers = lax.axis_size("dp")
    rows_dev, width = embeddings.shape
    slot = 2 * rows_dev // peers
    slots = peers * slot
    sems = pltpu.SemaphoreType.DMA((peers,))
    vmem = pl.BlockSpec(memory_space=pltpu.VMEM)
    return pl.pallas_call(
        functools.partial(smooth_kernel, peers, slot),
        out_shape=jax.ShapeDtypeStruct((rows_dev, width), jnp.bfloat16),
        in_specs=[pl.BlockSpec(memory_space=pl.ANY), vmem, vmem],
        out_specs=vmem,
        scratch_shapes=[
            pltpu.VMEM((rows_dev, width), jnp.bfloat16),
            pltpu.VMEM((slots, width), jnp.bfloat16),
            pltpu.VMEM((slots, width), jnp.bfloat16),
            pltpu.VMEM((slots, width), jnp.bfloat16),
            pltpu.VMEM((slots, width), jnp.bfloat16),
            pltpu.VMEM((slots, width), jnp.bfloat16),
            pltpu.VMEM((slots, rows_dev), jnp.bfloat16),
            pltpu.VMEM((1, slots), jnp.int32),
            pltpu.VMEM((peers, 1, slots), jnp.int32),
            pltpu.SemaphoreType.DMA,
            sems, sems, sems, sems, sems, sems,
        ],
        compiler_params=pltpu.CompilerParams(
            collective_id=0, has_side_effects=True, vmem_limit_bytes=32 * 1024 * 1024
        ),
    )(embeddings, cluster_ids.reshape(1, rows_dev), owner.reshape(1, -1))


def shards(embeddings, cluster_ids, owner):
    slot = 2 * embeddings.shape[0] // lax.axis_size("dp")
    if slot % ROW_TILE == 0:
        return by_kernel(embeddings, cluster_ids, owner)
    return by_collectives(embeddings, cluster_ids, owner)


def solution(mesh):
    placed = (P(("groups", "dp"), None), P(("groups", "dp")), P("groups"))
    return jax.shard_map(
        shards, mesh=mesh, in_specs=placed, out_specs=P(("groups", "dp"), None), check_vma=False
    )
```
